32 devices in a mesh: ep: 16 (over z, y, core), dp: 2 (over x).
Axes of the slice: x: 2, y: 2, z: 4, core: 2. Of those that a mesh axis runs over, the one named last changes fastest.
Arguments:
- tokens: bfloat16 [2, 128, 3584], P(None, ('ep', 'dp')), may hold values from -6 to 6
- routing: int32 [2, 128, 8], P(None, 'ep'), may hold values from 0 to 15, all different within a row; in each aligned block of 8 rows (0 to 7, 8 to 15, ..., all dimensions but the last counted through in order) at most 8 rows name the same one
- gate_values: float32 [2, 128, 8], P(None, 'ep'), may hold values from 0.05 to 0.5
- held_weight: bfloat16 [16, 3584, 1024], P('ep', None, 'dp'), may hold values from -0.09375 to 0.09375
- scale_table: float32 [16, 28, 8], P(None, None, 'dp'), may hold values from 0.25 to 4
- old_expert: int32 [16], replicated, may hold values from 0 to 15, as said below
- new_expert: int32 [16], replicated, may hold values from 0 to 15, as said below
Outputs:
- combined: bfloat16 [2, 128, 1024], P(None, 'ep', 'dp')
- moved_weight: bfloat16 [16, 3584, 1024], P('ep', None, 'dp')
The draws below stay inside these ranges and needn't reach their ends.
Inputs may be any that keep to these rules, and one draw needn't show every extreme that they name: `routing`: each row names 8 different experts; in each aligned block of 8 token rows of a step no expert is named by more than 8 rows. `old_expert`: A permutation of the experts over the slots. `new_expert`: A permutation of the experts over the slots; it equals old_expert except at exactly 4 slots, whose experts are permuted among themselves so that each of them changes.
All inputs are finite; a program needn't handle non-finite values.
Results may differ from the reference program's by a relative error of at most 0.0039.
Values may be sent and summed in bfloat16 or wider, within the bound.
A program may use at most 64 MiB of HBM per device.

```python
import math
import jax
import jax.numpy as jnp
import numpy as np
from jax import lax

D = 3584
FF = 1024
BLK = 128
TOP = 8
STEPS = 2
TOK_DEV = 4
EXPERTS = 16
TOKENS = 128
CAP = 8
MOVED = 4
N_DP = 2


def placement_pair(key):
    base = jax.random.fold_in(key, 11)
    first_key, second_key = jax.random.split(base)
    old_expert = jax.random.permutation(first_key, EXPERTS).astype(jnp.int32)
    chosen = jax.random.permutation(second_key, EXPERTS)[:MOVED]
    new_expert = old_expert.at[chosen].set(old_expert[jnp.roll(chosen, 1)])
    return (old_expert, new_expert.astype(jnp.int32))


def draw_old_expert(key, part):
    return placement_pair(key)[0]


def draw_new_expert(key, part):
    return placement_pair(key)[1]


def level_of(key, shape, cuts, low, largest):
    factor_of, own = 1.0, jax.random.fold_in(key, 6)
    for position, blocks in cuts:
        heights = jnp.exp(jax.random.uniform(jax.random.fold_in(own, position), (blocks,), jnp.float32, low / len(cuts), largest / len(cuts)))
        factor_of = factor_of * jnp.repeat(heights, shape[position] // blocks).reshape([-1 if axis == position else 1 for axis in range(len(shape))])
    return factor_of


def routed_block(own_key, own, number, rows, count, top, bound, lean):
    sequence = jax.random.permutation(own_key, count)
    heavy_load, common = shares(count, rows * top, bound, lean, True), shares(count, rows * top, bound, lean, False)
    places = jnp.arange(count)

    def named(lengths, offset_by):
        used = int((lengths > 0).sum())
        fixed = max(1, used // 4)
        moved = fixed + (places - fixed + offset_by * (used - fixed)) % max(1, count - fixed)
        return jnp.zeros((count,), jnp.int32).at[sequence[jnp.where(places < fixed, places, moved)]].set(jnp.asarray(lengths, jnp.int32))

    lengths = jnp.where(number % 4 == 0, named(heavy_load, number // 4), named(common, number - number // 4 - 1))
    mixed = jax.random.permutation(jax.random.fold_in(own, 3), count)
    source_of, taker = mixed[0:count // 2 * 2:2], mixed[1:count // 2 * 2:2]
    room = jnp.minimum(lengths[source_of] - 1, bound - lengths[taker]) // 2
    room = jnp.where((source_of == sequence[0]) | (taker == sequence[0]) | (lengths[taker] == 0), 0, jnp.maximum(room, 0))
    moved = jax.random.randint(jax.random.fold_in(own, 4), (count // 2,), 0, 1 << 20) % (room + 1)
    lengths = lengths.at[source_of].add(-moved).at[taker].add(moved)
    members = jnp.searchsorted(jnp.cumsum(lengths), jnp.arange(rows * top), side="right").astype(jnp.int32)
    grid = members.reshape(top, rows).T
    grid = grid[jax.random.permutation(jax.random.fold_in(own, 1), rows)]
    offset_by = jax.random.randint(jax.random.fold_in(own, 2), (rows, 1), 0, top)
    return jnp.take_along_axis(grid, (jnp.arange(top)[None, :] + offset_by) % top, axis=1)


def shares(amount, total, limit, slope, full):
    weights = [(1 << 20) // math.isqrt(rank ** slope) + 1 for rank in range(1, amount + 1)]
    largest = limit if full else min(limit, max(-(-total // amount), total * weights[0] // sum(weights)))
    least = 1 if total - largest >= amount - 1 else 0
    given, surplus = [largest] + [least] * (amount - 1), total - largest - least * (amount - 1)
    while surplus > 0:
        candidates = [i for i in range(1, amount) if given[i] < largest] or [i for i in range(1, amount) if given[i] < limit]
        whole, left = sum([weights[i] for i in candidates]), surplus
        for i in candidates:
            addition = min(limit - given[i], max(1, left * weights[i] // whole), surplus)
            given[i] = given[i] + addition
            surplus = surplus - addition
    return np.array(given)


def scatter_about(stream_key, dims, spread, bound, pieces=(), kind=jnp.bfloat16):
    array = spread * jax.random.normal(stream_key, dims, jnp.float32)
    if pieces:
        array = array * level_of(stream_key, dims, pieces, -0.22, 0.18)
    return jnp.clip(array, -bound, bound).astype(kind)


def setup_inputs(seed: int = 0) -> dict:
    keys = jax.random.split(jax.random.key(seed), 8)
    tokens = scatter_about(keys[0], (STEPS, TOKENS, D), 1.0, 6.0, ((1, 32),))
    routing_keys = jax.random.split(jax.random.fold_in(keys[1], 1), STEPS * TOKENS // (N_DP * TOK_DEV))
    routing_turns = jax.random.permutation(jax.random.fold_in(keys[1], 3), STEPS * TOKENS // (N_DP * TOK_DEV))
    routing = jax.vmap(lambda own, number: routed_block(jax.random.fold_in(keys[1], 2), own, number, N_DP * TOK_DEV, EXPERTS, TOP, CAP, 2))(routing_keys, routing_turns).reshape((STEPS, TOKENS, TOP))
    gate_values = jnp.clip(0.05 + 0.45 * jax.random.uniform(keys[2], (STEPS, TOKENS, TOP), jnp.float32) ** level_of(keys[2], (STEPS, TOKENS, TOP), ((1, 16),), -0.2, 0.2), 0.05, 0.5)
    held_weight = scatter_about(keys[3], (EXPERTS, D, FF), D ** -0.5, 0.09375, ((0, 16), (2, 2)))
    scale_table = jnp.clip(jnp.exp(math.log(4.0) - 2.7725887 * jax.random.uniform(keys[4], (EXPERTS, D // BLK, FF // BLK), jnp.float32) ** level_of(keys[4], (EXPERTS, D // BLK, FF // BLK), ((2, 2),), -0.2, 0.2)), 0.25, 4.0)
    old_expert = draw_old_expert(jax.random.fold_in(keys[7], 71), 0)
    new_expert = draw_new_expert(jax.random.fold_in(keys[7], 71), 0)
    return {"tokens": tokens, "routing": routing, "gate_values": gate_values, "held_weight": held_weight, "scale_table": scale_table, "old_expert": old_expert, "new_expert": new_expert}


def inverse_place(expert_at):
    count = expert_at.shape[0]
    labels = jnp.arange(count, dtype=jnp.int32)
    match = expert_at[None, :] == labels[:, None]
    return jnp.sum(jnp.where(match, labels[None, :], 0), axis=1).astype(jnp.int32)


def dequantized(weight_block, scales):
    widened = jnp.repeat(jnp.repeat(scales, BLK, axis=0), BLK, axis=1)
    return weight_block.astype(jnp.float32) * widened


def decode_once(token_rows, routing, gate_values, held_weight, owners, scale_table):
    group_size = N_DP * TOK_DEV
    group_count = TOKENS // group_size
    pair_ids = routing.reshape(-1).astype(jnp.int32)
    pair_total = pair_ids.shape[0]
    labels = jnp.arange(EXPERTS, dtype=jnp.int32)
    onehot = (pair_ids[:, None] == labels[None, :]).astype(jnp.int32)
    onehot = onehot.reshape(group_count, group_size * TOP, EXPERTS)
    before = jnp.cumsum(onehot, axis=1) - onehot
    slot_rank = jnp.sum(before * onehot, axis=2).reshape(-1).astype(jnp.int32)
    pair_index = jnp.arange(pair_total, dtype=jnp.int32)
    group_index = (pair_index // (group_size * TOP)).astype(jnp.int32)
    slot_table = jnp.full((EXPERTS, group_count, CAP), -1, jnp.int32)
    slot_table = slot_table.at[pair_ids, group_index, slot_rank].set(pair_index)
    flat_gates = gate_values.reshape(-1)

    def visit_expert(combined, expert):
        slot_pairs = slot_table[expert].reshape(-1)
        live_slot = slot_pairs >= 0
        safe_slot = jnp.where(live_slot, slot_pairs, 0).astype(jnp.int32)
        token_index = (safe_slot // TOP).astype(jnp.int32)
        features = token_rows[token_index].astype(jnp.float32)
        weights = dequantized(held_weight[owners[expert]], scale_table[expert])
        hidden = jnp.dot(features, weights, precision=lax.Precision.HIGHEST, preferred_element_type=jnp.float32)
        rounded = lax.optimization_barrier(jax.nn.silu(hidden).astype(jnp.bfloat16))
        activated = rounded.astype(jnp.float32)
        weighted = jnp.where(live_slot[:, None], flat_gates[safe_slot][:, None] * activated, jnp.float32(0.0))
        return combined.at[token_index].add(weighted), None

    start = jnp.zeros((TOKENS, FF), jnp.float32)
    combined, _ = lax.scan(visit_expert, start, jnp.arange(EXPERTS, dtype=jnp.int32))
    return combined


def reference(tokens, routing, gate_values, held_weight, scale_table, old_expert, new_expert):
    owners = inverse_place(old_expert)
    moved_weight = held_weight[owners[new_expert]]
    results = []
    for decode_step in range(STEPS):
        results.append(decode_once(tokens[decode_step], routing[decode_step], gate_values[decode_step], held_weight, owners, scale_table))
    return jnp.stack(results).astype(jnp.bfloat16), moved_weight
```

```python
import functools

import jax
import jax.numpy as jnp
import numpy as np
from jax import lax
from jax.experimental import pallas as pl
from jax.experimental.pallas import tpu as pltpu
from jax.sharding import PartitionSpec as P

MESH = pl.DeviceIdType.MESH
MOVED_BITS = 4
CHUNKS = 2


def inverse_place(expert_at):
    count = expert_at.shape[0]
    labels = jnp.arange(count, dtype=jnp.int32)
    match = expert_at[None, :] == labels[:, None]
    return jnp.sum(jnp.where(match, labels[None, :], 0), axis=1)


def source_slots(old_expert, new_expert):
    labels = jnp.arange(old_expert.shape[0], dtype=jnp.int32)
    match = old_expert[None, :] == new_expert[:, None]
    return jnp.sum(jnp.where(match, labels[None, :], 0), axis=1)


def parity(number):
    return bin(number).count("1") % 2


def halves():
    return [(mask, side) for mask in range(1, 16) for side in range(2)]


def half_members(mask, side):
    return [s for s in range(16) if parity(s & mask) == side]


def free_bits(mask):
    pivot = min(j for j in range(MOVED_BITS) if mask >> j & 1)
    return [j for j in range(MOVED_BITS) if j != pivot]


def rank_in_half(mask, slot):
    return sum((slot >> j & 1) << i for i, j in enumerate(free_bits(mask)))


def relocate_kernel(mask, side, ranks_ref, x_ref, o_ref, *scratch):
    got, stage = scratch[:CHUNKS], scratch[CHUNKS : 2 * CHUNKS]
    send_sem, recv_sem, own_sem = scratch[2 * CHUNKS :]
    me = lax.axis_index("ep")
    bits = [lax.rem(me // (1 << j), 2) for j in range(MOVED_BITS)]
    flips = [1 - 2 * bit for bit in bits]
    my_parity = lax.rem(sum(bits[j] for j in range(MOVED_BITS) if mask >> j & 1), 2)
    kept = free_bits(mask)
    rank = sum(bits[j] * (1 << i) for i, j in enumerate(kept))
    turns = [t for t in range(1, 16) if parity(t & mask) == 0]

    def partner(turn):
        slot = me + sum(flips[j] * (1 << j) for j in range(MOVED_BITS) if turn >> j & 1)
        its_rank = rank + sum(flips[j] * (1 << i) for i, j in enumerate(kept) if turn >> j & 1)
        return slot, its_rank

    @pl.when(my_parity != side)
    def _():
        copy = pltpu.make_async_copy(x_ref, o_ref, own_sem.at[0, 0])
        copy.start()
        copy.wait()

    @pl.when(my_parity == side)
    def _():
        def scatter(chunk, i, turn):
            slot, its_rank = partner(turn)
            return pltpu.make_async_remote_copy(
                src_ref=x_ref.at[its_rank, chunk],
                dst_ref=got[chunk].at[rank],
                send_sem=send_sem.at[0, chunk, i],
                recv_sem=recv_sem.at[0, chunk, i],
                device_id={"ep": slot},
                device_id_type=MESH,
            )

        def gather(chunk, i, turn):
            slot, its_rank = partner(turn)
            return pltpu.make_async_remote_copy(
                src_ref=stage[chunk].at[its_rank],
                dst_ref=o_ref.at[rank, chunk],
                send_sem=send_sem.at[1, chunk, i],
                recv_sem=recv_sem.at[1, chunk, i],
                device_id={"ep": slot},
                device_id_type=MESH,
            )

        def own_in(chunk):
            return pltpu.make_async_copy(x_ref.at[rank, chunk], got[chunk].at[rank], own_sem.at[0, chunk])

        def own_out(chunk):
            return pltpu.make_async_copy(stage[chunk].at[rank], o_ref.at[rank, chunk], own_sem.at[1, chunk])

        for chunk in range(CHUNKS):
            for i, turn in enumerate(turns):
                scatter(chunk, i, turn).start()
            own_in(chunk).start()
        for chunk in range(CHUNKS):
            own_in(chunk).wait()
            for i, turn in enumerate(turns):
                scatter(chunk, i, turn).wait_recv()

            def place(index, carry, chunk=chunk):
                stage[chunk][index] = got[chunk][ranks_ref[index]]
                return carry

            lax.fori_loop(0, 8, place, 0)
            for i, turn in enumerate(turns):
                gather(chunk, i, turn).start()
            own_out(chunk).start()
        for chunk in range(CHUNKS):
            own_out(chunk).wait()
            for i, turn in enumerate(turns):
                scatter(chunk, i, turn).wait_send()
                gather(chunk, i, turn).wait()


def relocate(old_block, old_expert, new_expert):
    depth, width = old_block.shape
    rows = depth // (8 * CHUNKS)
    sources = source_slots(old_expert, new_expert)
    moved = (old_expert != new_expert).astype(jnp.int32)
    table = np.array([[parity(s & mask) == side for s in range(16)] for mask, side in halves()], np.int32)
    chosen = jnp.argmax(jnp.sum(jnp.asarray(table) * moved[None, :], axis=1)).astype(jnp.int32)

    def branch(mask, side):
        members = np.array(half_members(mask, side), np.int32)
        members = members[np.argsort([rank_in_half(mask, s) for s in members])]
        rank_of = np.array([rank_in_half(mask, s) for s in range(16)], np.int32)

        def run(block, sources):
            ranks = jnp.asarray(rank_of)[sources[members]]
            piece = (8, rows, width)
            return pl.pallas_call(
                functools.partial(relocate_kernel, mask, side),
                out_shape=jax.ShapeDtypeStruct((8, CHUNKS, rows, width), block.dtype),
                in_specs=[pl.BlockSpec(memory_space=pltpu.SMEM), pl.BlockSpec(memory_space=pl.ANY)],
                out_specs=pl.BlockSpec(memory_space=pl.ANY),
                scratch_shapes=[pltpu.VMEM(piece, block.dtype)] * (2 * CHUNKS)
                + [
                    pltpu.SemaphoreType.DMA((2, CHUNKS, 7)),
                    pltpu.SemaphoreType.DMA((2, CHUNKS, 7)),
                    pltpu.SemaphoreType.DMA((2, CHUNKS)),
                ],
                compiler_params=pltpu.CompilerParams(has_side_effects=True, vmem_limit_bytes=32 << 20),
                name=f"relocate_{mask}_{side}",
            )(ranks, block)

        return run

    pieces = old_block.reshape(8, CHUNKS, rows, width)
    moved_pieces = lax.switch(chosen, [branch(*half) for half in halves()], pieces, sources)
    return moved_pieces.reshape(depth, width)


def serve_kernel(steps, block_rows, blocks, x_ref, w_ref, s_ref, o_ref, total):
    step = pl.program_id(0)

    @pl.when(step == 0)
    def _():
        total[...] = jnp.zeros_like(total)

    value = total[...]
    for i in range(blocks):
        rows = pl.ds(i * block_rows, block_rows)
        product = jnp.dot(x_ref[:, rows], w_ref[rows, :], preferred_element_type=jnp.float32)
        value = value + product * s_ref[0, i : i + 1, :]
    total[...] = value

    @pl.when(step == steps - 1)
    def _():
        u = total[...]
        o_ref[...] = (u / (1.0 + jnp.exp(-u))).astype(o_ref.dtype)


def serve(rows, block, scales):
    count, depth = rows.shape
    width = block.shape[1]
    row_blocks = scales.shape[0]
    block_rows = depth // row_blocks
    blocks = 4
    steps = row_blocks // blocks
    widened = jnp.repeat(scales, width // scales.shape[1], axis=1).reshape(steps, blocks, width)
    return pl.pallas_call(
        functools.partial(serve_kernel, steps, block_rows, blocks),
        out_shape=jax.ShapeDtypeStruct((count, width), jnp.bfloat16),
        grid=(steps,),
        in_specs=[
            pl.BlockSpec((count, blocks * block_rows), lambda i: (0, i)),
            pl.BlockSpec((blocks * block_rows, width), lambda i: (i, 0)),
            pl.BlockSpec((1, blocks, width), lambda i: (i, 0, 0)),
        ],
        out_specs=pl.BlockSpec((count, width), lambda i: (0, 0)),
        scratch_shapes=[pltpu.VMEM((count, width), jnp.float32)],
        compiler_params=pltpu.CompilerParams(vmem_limit_bytes=32 << 20),
        cost_estimate=pl.CostEstimate(
            flops=2 * count * depth * width, bytes_accessed=2 * depth * (count + width), transcendentals=count * width
        ),
        name="serve",
    )(rows, block, widened)


def relocate_any(old_block, old_expert, new_expert):
    peers = lax.axis_size("ep")
    sources = source_slots(old_expert, new_expert)
    pieces = old_block.reshape(peers, old_block.shape[0] // peers, old_block.shape[1])
    gathered = lax.all_to_all(pieces, "ep", split_axis=0, concat_axis=0, tiled=True)
    placed = lax.map(lambda s: lax.dynamic_index_in_dim(gathered, s, keepdims=False), sources)
    return lax.all_to_all(placed, "ep", split_axis=0, concat_axis=0, tiled=True).reshape(old_block.shape)


def served(tokens, routing, gate_values, old_block, scales, old_expert):
    peers = lax.axis_size("ep")
    steps, group, _ = routing.shape
    depth, width = old_block.shape
    everyone = lax.all_gather(tokens, ("ep", "dp"), axis=1, tiled=True)
    act = serve(everyone.reshape(-1, depth), old_block, scales).reshape(steps, peers, group, width)
    returned = lax.all_to_all(act, "ep", split_axis=1, concat_axis=1, tiled=True)
    gates = jnp.sum(
        jnp.where(old_expert[None, None, None, :] == routing[..., None], gate_values[..., None], 0.0), axis=2
    )
    weighted = jnp.sum(jnp.transpose(gates, (0, 2, 1))[..., None] * returned.astype(jnp.float32), axis=1)
    return weighted.astype(jnp.bfloat16)


def shards(tokens, routing, gate_values, held_weight, scale_table, old_expert, new_expert):
    old_block = held_weight[0]
    scales = scale_table[old_expert[lax.axis_index("ep")]]
    if lax.axis_size("ep") == 16:
        combined = served(tokens, routing, gate_values, old_block, scales, old_expert)
        new_block = relocate(old_block, old_expert, new_expert)
    else:
        done = []
        for n in range(tokens.shape[0]):
            step = (tokens[n : n + 1], routing[n : n + 1], gate_values[n : n + 1])
            if done:
                step, done[-1] = lax.optimization_barrier((step, done[-1]))
            done.append(served(*step, old_block, scales, old_expert))
        combined = jnp.concatenate(done)
        new_block = relocate_any(old_block, old_expert, new_expert)
    return combined, new_block[None]


def solution(mesh):
    placed = (
        P(None, ("ep", "dp"), None),
        P(None, "ep", None),
        P(None, "ep", None),
        P("ep", None, "dp"),
        P(None, None, "dp"),
        P(),
        P(),
    )
    return jax.shard_map(
        shards,
        mesh=mesh,
        in_specs=placed,
        out_specs=(P(None, "ep", "dp"), P("ep", None, "dp")),
        check_vma=False,
    )
```

```python
import functools

import jax
import jax.numpy as jnp
import numpy as np
from jax import lax
from jax.experimental import pallas as pl
from jax.experimental.pallas import tpu as pltpu
from jax.sharding import PartitionSpec as P

MESH = pl.DeviceIdType.MESH
MOVED_BITS = 4
CHUNKS = 2


def inverse_place(expert_at):
    count = expert_at.shape[0]
    labels = jnp.arange(count, dtype=jnp.int32)
    match = expert_at[None, :] == labels[:, None]
    return jnp.sum(jnp.where(match, labels[None, :], 0), axis=1)


def source_slots(old_expert, new_expert):
    labels = jnp.arange(old_expert.shape[0], dtype=jnp.int32)
    match = old_expert[None, :] == new_expert[:, None]
    return jnp.sum(jnp.where(match, labels[None, :], 0), axis=1)


def parity(number):
    return bin(number).count("1") % 2


def halves():
    masks = sorted(range(1, 16), key=lambda mask: (mask in (2, 10), mask))
    return [(mask, side) for mask in masks for side in range(2)]


def free_bits(mask):
    pivot = min(j for j in range(MOVED_BITS) if mask >> j & 1)
    return [j for j in range(MOVED_BITS) if j != pivot]


def relocate_kernel(mask, side, sources_ref, x_ref, o_ref, *scratch):
    got, stage = scratch[:CHUNKS], scratch[CHUNKS : 2 * CHUNKS]
    send_sem, recv_sem, own_sem = scratch[2 * CHUNKS :]
    me = lax.axis_index("ep")
    bits = [lax.rem(me // (1 << j), 2) for j in range(MOVED_BITS)]
    flips = [1 - 2 * bit for bit in bits]
    my_parity = lax.rem(sum(bits[j] for j in range(MOVED_BITS) if mask >> j & 1), 2)
    kept = free_bits(mask)
    rank = sum(bits[j] * (1 << i) for i, j in enumerate(kept))
    turns = [t for t in range(1, 16) if parity(t & mask) == 0]

    def partner(turn):
        slot = me + sum(flips[j] * (1 << j) for j in range(MOVED_BITS) if turn >> j & 1)
        its_rank = rank + sum(flips[j] * (1 << i) for i, j in enumerate(kept) if turn >> j & 1)
        return slot, its_rank

    def source_rank(index):
        pivot = min(j for j in range(MOVED_BITS) if mask >> j & 1)
        digits = {j: lax.rem(index // (1 << i), 2) for i, j in enumerate(kept)}
        digits[pivot] = lax.rem(side + sum(digits[j] for j in kept if mask >> j & 1), 2)
        source = sources_ref[sum(digits[j] * (1 << j) for j in range(MOVED_BITS))]
        return sum(lax.rem(source // (1 << j), 2) * (1 << i) for i, j in enumerate(kept))

    @pl.when(my_parity != side)
    def _():
        def pass_in(chunk):
            return pltpu.make_async_copy(x_ref.at[:, chunk], got[chunk], own_sem.at[0, chunk])

        def pass_out(chunk):
            return pltpu.make_async_copy(got[chunk], o_ref.at[:, chunk], own_sem.at[1, chunk])

        for chunk in range(CHUNKS):
            pass_in(chunk).start()
        for chunk in range(CHUNKS):
            pass_in(chunk).wait()
            pass_out(chunk).start()
        for chunk in range(CHUNKS):
            pass_out(chunk).wait()

    @pl.when(my_parity == side)
    def _():
        def scatter(chunk, i, turn):
            slot, its_rank = partner(turn)
            return pltpu.make_async_remote_copy(
                src_ref=x_ref.at[its_rank, chunk],
                dst_ref=got[chunk].at[rank],
                send_sem=send_sem.at[0, chunk, i],
                recv_sem=recv_sem.at[0, chunk, i],
                device_id={"ep": slot},
                device_id_type=MESH,
            )

        def gather(chunk, i, turn):
            slot, its_rank = partner(turn)
            return pltpu.make_async_remote_copy(
                src_ref=stage[chunk].at[its_rank],
                dst_ref=o_ref.at[rank, chunk],
                send_sem=send_sem.at[1, chunk, i],
                recv_sem=recv_sem.at[1, chunk, i],
                device_id={"ep": slot},
                device_id_type=MESH,
            )

        def own_in(chunk):
            return pltpu.make_async_copy(x_ref.at[rank, chunk], got[chunk].at[rank], own_sem.at[0, chunk])

        def own_out(chunk):
            return pltpu.make_async_copy(stage[chunk].at[rank], o_ref.at[rank, chunk], own_sem.at[1, chunk])

        for chunk in range(CHUNKS):
            for i, turn in enumerate(turns):
                scatter(chunk, i, turn).start()
            own_in(chunk).start()
        for chunk in range(CHUNKS):
            own_in(chunk).wait()
            for i, turn in enumerate(turns):
                scatter(chunk, i, turn).wait_recv()

            def place(index, carry, chunk=chunk):
                stage[chunk][index] = got[chunk][source_rank(index)]
                return carry

            lax.fori_loop(0, 8, place, 0)
            for i, turn in enumerate(turns):
                gather(chunk, i, turn).start()
            own_out(chunk).start()
        for chunk in range(CHUNKS):
            own_out(chunk).wait()
            for i, turn in enumerate(turns):
                scatter(chunk, i, turn).wait_send()
                gather(chunk, i, turn).wait()


def relocate(old_block, old_expert, new_expert):
    depth, width = old_block.shape
    rows = depth // (8 * CHUNKS)
    sources = source_slots(old_expert, new_expert)
    moved = (old_expert != new_expert).astype(jnp.int32)
    table = np.array([[parity(s & mask) == side for s in range(16)] for mask, side in halves()], np.int32)
    chosen = jnp.argmax(jnp.sum(jnp.asarray(table) * moved[None, :], axis=1)).astype(jnp.int32)

    def branch(mask, side):
        def run(block, sources):
            piece = (8, rows, width)
            return pl.pallas_call(
                functools.partial(relocate_kernel, mask, side),
                out_shape=jax.ShapeDtypeStruct((8, CHUNKS, rows, width), block.dtype),
                in_specs=[pl.BlockSpec(memory_space=pltpu.SMEM), pl.BlockSpec(memory_space=pl.ANY)],
                out_specs=pl.BlockSpec(memory_space=pl.ANY),
                scratch_shapes=[pltpu.VMEM(piece, block.dtype)] * (2 * CHUNKS)
                + [
                    pltpu.SemaphoreType.DMA((2, CHUNKS, 7)),
                    pltpu.SemaphoreType.DMA((2, CHUNKS, 7)),
                    pltpu.SemaphoreType.DMA((2, CHUNKS)),
                ],
                compiler_params=pltpu.CompilerParams(has_side_effects=True, vmem_limit_bytes=32 << 20),
                name=f"relocate_{mask}_{side}",
            )(sources, block)

        return run

    pieces = old_block.reshape(8, CHUNKS, rows, width)
    moved_pieces = lax.switch(chosen, [branch(*half) for half in halves()], pieces, sources)
    return moved_pieces.reshape(depth, width)


def serve_kernel(steps, block_rows, blocks, x_ref, w_ref, s_ref, *rest):
    *passed, total = rest
    o_ref = passed[-1]
    step = pl.program_id(0)
    if len(passed) == 3:
        passed[1][...] = passed[0][...]

    @pl.when(step == 0)
    def _():
        total[...] = jnp.zeros_like(total)

    value = total[...]
    for i in range(blocks):
        rows = pl.ds(i * block_rows, block_rows)
        product = jnp.dot(x_ref[:, rows], w_ref[rows, :], preferred_element_type=jnp.float32)
        value = value + product * s_ref[0, i : i + 1, :]
    total[...] = value

    @pl.when(step == steps - 1)
    def _():
        u = total[...]
        o_ref[...] = (u / (1.0 + jnp.exp(-u))).astype(o_ref.dtype)


def serve(rows, block, scales, moved=None):
    count, depth = rows.shape
    width = block.shape[1]
    row_blocks = scales.shape[0]
    block_rows = depth // row_blocks
    blocks = 4
    steps = row_blocks // blocks
    widened = jnp.repeat(scales, width // scales.shape[1], axis=1).reshape(steps, blocks, width)
    weights = pl.BlockSpec((blocks * block_rows, width), lambda i: (i, 0))
    act = jax.ShapeDtypeStruct((count, width), jnp.bfloat16)
    act_spec = pl.BlockSpec((count, width), lambda i: (0, 0))
    extra = [] if moved is None else [moved]
    return pl.pallas_call(
        functools.partial(serve_kernel, steps, block_rows, blocks),
        out_shape=[jax.ShapeDtypeStruct(e.shape, e.dtype) for e in extra] + [act],
        grid=(steps,),
        in_specs=[
            pl.BlockSpec((count, blocks * block_rows), lambda i: (0, i)),
            weights,
            pl.BlockSpec((1, blocks, width), lambda i: (i, 0, 0)),
        ]
        + [weights] * len(extra),
        out_specs=[weights] * len(extra) + [act_spec],
        scratch_shapes=[pltpu.VMEM((count, width), jnp.float32)],
        compiler_params=pltpu.CompilerParams(vmem_limit_bytes=32 << 20),
        cost_estimate=pl.CostEstimate(
            flops=2 * count * depth * width,
            bytes_accessed=2 * depth * (count + (1 + 2 * len(extra)) * width),
            transcendentals=count * width,
        ),
        name="serve",
    )(rows, block, widened, *extra)


def relocate_any(old_block, old_expert, new_expert):
    peers = lax.axis_size("ep")
    sources = source_slots(old_expert, new_expert)
    pieces = old_block.reshape(peers, old_block.shape[0] // peers, old_block.shape[1])
    gathered = lax.all_to_all(pieces, "ep", split_axis=0, concat_axis=0, tiled=True)
    placed = lax.map(lambda s: lax.dynamic_index_in_dim(gathered, s, keepdims=False), sources)
    return lax.all_to_all(placed, "ep", split_axis=0, concat_axis=0, tiled=True).reshape(old_block.shape)


def served(tokens, routing, gate_values, old_block, scales, old_expert, moved=None):
    peers = lax.axis_size("ep")
    steps, group, _ = routing.shape
    depth, width = old_block.shape
    mine = jnp.transpose(tokens, (1, 0, 2)).reshape(-1, depth)
    everyone = lax.all_gather(mine, ("ep", "dp"), axis=0, tiled=True)
    *passed, act = serve(everyone, old_block, scales, moved)
    act = act.reshape(peers, group * steps, width)
    returned = lax.all_to_all(act, "ep", split_axis=0, concat_axis=0, tiled=True)
    gates = jnp.sum(
        jnp.where(old_expert[:, None, None, None] == routing[None], gate_values[None], 0.0), axis=3
    )
    gates = jnp.transpose(gates, (0, 2, 1)).reshape(peers, group * steps)
    weighted = jnp.sum(gates[:, :, None] * returned.astype(jnp.float32), axis=0)
    weighted = weighted.astype(jnp.bfloat16).reshape(group, steps, width)
    return jnp.transpose(weighted, (1, 0, 2)), *passed


def shards(tokens, routing, gate_values, held_weight, scale_table, old_expert, new_expert):
    old_block = held_weight[0]
    scales = scale_table[old_expert[lax.axis_index("ep")]]
    if lax.axis_size("ep") == 16:
        new_block = relocate(old_block, old_expert, new_expert)
        combined, new_block = served(
            tokens, routing, gate_values, old_block, scales, old_expert, new_block
        )
    else:
        done = []
        for n in range(tokens.shape[0]):
            step = (tokens[n : n + 1], routing[n : n + 1], gate_values[n : n + 1])
            if done:
                step, done[-1] = lax.optimization_barrier((step, done[-1]))
            done += served(*step, old_block, scales, old_expert)
        combined = jnp.concatenate(done)
        new_block = relocate_any(old_block, old_expert, new_expert)
    return combined, new_block[None]


def solution(mesh):
    placed = (
        P(None, ("ep", "dp"), None),
        P(None, "ep", None),
        P(None, "ep", None),
        P("ep", None, "dp"),
        P(None, None, "dp"),
        P(),
        P(),
    )
    return jax.shard_map(
        shards,
        mesh=mesh,
        in_specs=placed,
        out_specs=(P(None, "ep", "dp"), P("ep", None, "dp")),
        check_vma=False,
    )
```
